32 devices in a mesh: dp: 2 (over y), expert: 16 (over z, x, core).
Axes of the slice: x: 2, y: 2, z: 4, core: 2. Of those that a mesh axis runs over, the one named last changes fastest.
Arguments:
- tokens: bfloat16 [4096, 2048], P(('dp', 'expert')), may hold values from -6 to 6
- out_grad: bfloat16 [4096, 2048], P(('dp', 'expert')), may hold values from -6 to 6
- routes: int32 [4096, 6], P(('dp', 'expert')), may hold values from 0 to 15, all different within a row; in each aligned block of 128 rows (0 to 127, 128 to 255, ...) at most 49 rows name the same one
- gate_weights: bfloat16 [4096, 6], P(('dp', 'expert')), may hold values from 0.049804688 to 0.59765625
- saved_preacts: bfloat16 [2, 16, 784, 1408], P('dp', 'expert'), may hold values from -6 to 6
- gate_up: bfloat16 [16, 2048, 1408], P('expert', 'dp'), may hold values from -0.125 to 0.125
- down_proj: bfloat16 [16, 704, 2048], P('expert', 'dp'), may hold values from -0.21875 to 0.21875
Outputs:
- grad_tokens: bfloat16 [4096, 2048], P(('dp', 'expert'))
- grad_gates: bfloat16 [4096, 6], P(('dp', 'expert'))
- grad_gate_up: float32 [16, 2048, 1408], P('expert', 'dp')
- grad_down: float32 [16, 704, 2048], P('expert', 'dp')
The draws below stay inside these ranges and needn't reach their ends.
Inputs may be any that keep to these rules, and one draw needn't show every extreme that they name: `routes`: each token names 6 different experts. Within the 128 rows of one device no expert is named by more than 49 rows, a bound that some block reaches.
All inputs are finite; a program needn't handle non-finite values.
Results may differ from the reference program's by a relative error of at most 0.0095.
Values may be sent and summed in bfloat16 or wider, within the bound.
No kernel may reach another device: no remote copies, remote signals or barrier semaphores. Data moves between devices by JAX's collectives and lax.ppermute only.
A program may use at most 128 MiB of HBM per device.

```python
import math
import jax
import jax.numpy as jnp
import numpy as np
from jax import lax

D = 2048
FF = 704
TOP = 6
TOK_DEV = 128
EXPERTS = 16
CAP = 49
TOKENS = 4096
ROUTE_COUNT = 1536
N_DP = 2


def level_of(rng, extent, split, low, largest):
    def one(dim, blocks):
        draws = jax.random.uniform(jax.random.fold_in(jax.random.fold_in(rng, 6), dim), (blocks,), jnp.float32, low / len(split), largest / len(split))
        return jnp.repeat(jnp.exp(draws), extent[dim] // blocks).reshape((-1,) + (1,) * (len(extent) - dim - 1))

    gain = one(*split[0])
    for cut in split[1:]:
        gain = gain * one(*cut)
    return gain


def assign_block(rng, own, number, rows, count, top, most, skew):
    sequence = jax.random.permutation(rng, count)
    crowded, usual = shares(count, rows * top, most, skew, True), shares(count, rows * top, most, skew, False)
    places = jnp.arange(count)

    def named(tallies, offset_by):
        used = int((tallies > 0).sum())
        fixed = max(1, used // 4)
        shifted = fixed + (places - fixed + offset_by * (used - fixed)) % max(1, count - fixed)
        return jnp.zeros((count,), jnp.int32).at[sequence[jnp.where(places < fixed, places, shifted)]].set(jnp.asarray(tallies, jnp.int32))

    tallies = jnp.where(number % 4 == 0, named(crowded, number // 4), named(usual, number - number // 4 - 1))
    mixed = jax.random.permutation(jax.random.fold_in(own, 3), count)
    donor, receiver = mixed[0:count // 2 * 2:2], mixed[1:count // 2 * 2:2]
    margin = jnp.minimum(tallies[donor] - 1, most - tallies[receiver]) // 2
    margin = jnp.where((donor == sequence[0]) | (receiver == sequence[0]) | (tallies[receiver] == 0), 0, jnp.maximum(margin, 0))
    shifted = jax.random.randint(jax.random.fold_in(own, 4), (count // 2,), 0, 1 << 20) % (margin + 1)
    tallies = tallies.at[donor].add(-shifted).at[receiver].add(shifted)
    labels = jnp.searchsorted(jnp.cumsum(tallies), jnp.arange(rows * top), side="right").astype(jnp.int32)
    grid = labels.reshape(top, rows).T
    grid = grid[jax.random.permutation(jax.random.fold_in(own, 1), rows)]
    offset_by = jax.random.randint(jax.random.fold_in(own, 2), (rows, 1), 0, top)
    return jnp.take_along_axis(grid, (jnp.arange(top)[None, :] + offset_by) % top, axis=1)


def shares(amount, total, most, skew, full):
    loads = [(1 << 20) // math.isqrt(standing ** skew) + 1 for standing in range(1, amount + 1)]
    largest = most if full else min(most, max(-(-total // amount), total * loads[0] // sum(loads)))
    least = 1 if total - largest >= amount - 1 else 0
    counts, rest = [largest] + [least] * (amount - 1), total - largest - least * (amount - 1)
    while rest > 0:
        movable = [i for i in range(1, amount) if counts[i] < largest] or [i for i in range(1, amount) if counts[i] < most]
        mass, remaining = sum([loads[i] for i in movable]), rest
        for i in movable:
            more = min(most - counts[i], max(1, remaining * loads[i] // mass), rest)
            counts[i] = counts[i] + more
            rest = rest - more
    return np.array(counts)


def bell_draw(key, dims, scale, bound, split=(), held_as=jnp.bfloat16):
    array = jax.random.normal(key, dims, jnp.float32) * scale
    if len(split) > 0:
        array = level_of(key, dims, split, -0.22, 0.18) * array
    return jnp.clip(array, min=-bound, max=bound).astype(held_as)


def setup_inputs(seed: int = 0) -> dict:
    arg_keys = jax.random.split(jax.random.key(seed), 8)
    tokens = bell_draw(arg_keys[0], (TOKENS, D), 1.0, 6.0, ((0, 32),))
    out_grad = bell_draw(arg_keys[1], (TOKENS, D), 1.0, 6.0, ((0, 32),))
    routes_keys = jax.random.split(jax.random.fold_in(arg_keys[2], 1), TOKENS // TOK_DEV)
    routes_turns = jax.random.permutation(jax.random.fold_in(arg_keys[2], 3), TOKENS // TOK_DEV)
    routes = jax.vmap(lambda own, number: assign_block(jax.random.fold_in(arg_keys[2], 2), own, number, TOK_DEV, EXPERTS, TOP, CAP, 2))(routes_keys, routes_turns).reshape((TOKENS, TOP))
    gate_weights = jnp.clip(jnp.exp(math.log(0.59765625) - 2.4849066 * jax.random.uniform(arg_keys[3], (TOKENS, TOP), jnp.float32) ** level_of(arg_keys[3], (TOKENS, TOP), ((0, 32),), -0.2, 0.2)), 0.049804688, 0.59765625).astype(jnp.bfloat16)
    saved_preacts = bell_draw(arg_keys[4], (N_DP, EXPERTS, EXPERTS * CAP, 2 * FF), 1.0, 6.0, ((0, 2), (1, 16)))
    gate_up = bell_draw(arg_keys[5], (EXPERTS, D, 2 * FF), D ** -0.5, 0.125, ((0, 16), (1, 2)))
    down_proj = bell_draw(arg_keys[6], (EXPERTS, FF, D), FF ** -0.5, 0.21875, ((0, 16), (1, 2)))
    return {"tokens": tokens, "out_grad": out_grad, "routes": routes, "gate_weights": gate_weights, "saved_preacts": saved_preacts, "gate_up": gate_up, "down_proj": down_proj}


def find_slots(route_block, capacity):
    flat = route_block.reshape(-1).astype(jnp.int32)
    onehot = (flat[:, None] == jnp.arange(EXPERTS, dtype=jnp.int32)[None, :]).astype(jnp.int32)
    before = jnp.cumsum(onehot, axis=0) - onehot
    position = lax.optimization_barrier(jnp.sum(before * onehot, axis=1)).astype(jnp.int32)
    return (flat * capacity + position).astype(jnp.int32)

def place_rows(values, slot_index):
    owner_row = jnp.arange(TOK_DEV * TOP, dtype=jnp.int32) // TOP
    empty = jnp.zeros((EXPERTS * CAP,) + values.shape[1:], values.dtype)
    return empty.at[slot_index].set(values[owner_row])

def expert_backward(operands):
    x_rows, dy_rows, g_rows, saved_rows, weights_gate_up, weights_down = operands
    gate_pre = saved_rows[:, :FF].astype(jnp.float32)
    up_pre = saved_rows[:, FF:].astype(jnp.float32)
    sigmoid_gate = jax.nn.sigmoid(gate_pre)
    act = (gate_pre * sigmoid_gate * up_pre).astype(jnp.bfloat16)
    act_grad = jnp.dot(dy_rows, weights_down.T, preferred_element_type=jnp.float32)
    gate_grad_rows = (lax.optimization_barrier(jnp.sum(act.astype(jnp.float32) * act_grad, axis=1)) / jnp.sqrt(jnp.float32(D))).astype(jnp.bfloat16)
    scaled_grad = g_rows.astype(jnp.float32)[:, None] * act_grad
    grad_gate = scaled_grad * up_pre * sigmoid_gate * (1.0 + gate_pre * (1.0 - sigmoid_gate))
    grad_up = scaled_grad * gate_pre * sigmoid_gate
    pre_grad = jnp.concatenate([grad_gate, grad_up], axis=1).astype(jnp.bfloat16)
    scaled_dy = (g_rows.astype(jnp.float32)[:, None] * dy_rows.astype(jnp.float32)).astype(jnp.bfloat16)
    row_grad = jnp.dot(pre_grad, weights_gate_up.T, preferred_element_type=jnp.float32).astype(jnp.bfloat16)
    grad_weights_gu = jnp.dot(x_rows.T, pre_grad, preferred_element_type=jnp.float32)
    grad_weights_down = jnp.dot(act.T, scaled_dy, preferred_element_type=jnp.float32)
    return (row_grad, gate_grad_rows, grad_weights_gu, grad_weights_down)

def reference(tokens, out_grad, routes, gate_weights, saved_preacts, gate_up, down_proj):
    tok_blocks = tokens.reshape(N_DP, EXPERTS, TOK_DEV, D)
    grad_blocks = out_grad.reshape(N_DP, EXPERTS, TOK_DEV, D)
    route_blocks = routes.reshape(N_DP, EXPERTS, TOK_DEV, TOP)
    gate_blocks = gate_weights.reshape(N_DP, EXPERTS, TOK_DEV * TOP)
    total_gu = jnp.zeros((EXPERTS, D, 2 * FF), jnp.float32)
    total_down = jnp.zeros((EXPERTS, FF, D), jnp.float32)
    token_grads = []
    gate_grads = []
    for replica in range(N_DP):
        slot_index = jax.vmap(lambda blk: find_slots(blk, CAP))(route_blocks[replica])
        send_x = jax.vmap(place_rows)(tok_blocks[replica], slot_index)
        send_dy = jax.vmap(place_rows)(grad_blocks[replica], slot_index)
        send_g = jax.vmap(lambda vals, idx: jnp.zeros((EXPERTS * CAP,), vals.dtype).at[idx].set(vals))(gate_blocks[replica], slot_index)
        recv_x = send_x.reshape(EXPERTS, EXPERTS, CAP, D).transpose(1, 0, 2, 3).reshape(EXPERTS, EXPERTS * CAP, D)
        recv_dy = send_dy.reshape(EXPERTS, EXPERTS, CAP, D).transpose(1, 0, 2, 3).reshape(EXPERTS, EXPERTS * CAP, D)
        recv_g = send_g.reshape(EXPERTS, EXPERTS, CAP).transpose(1, 0, 2).reshape(EXPERTS, EXPERTS * CAP)
        row_grad, gate_grad_rows, grad_gu, grad_dn = lax.map(expert_backward, (recv_x, recv_dy, recv_g, saved_preacts[replica], gate_up, down_proj))
        total_gu = total_gu + grad_gu
        total_down = total_down + grad_dn
        back_rows = row_grad.reshape(EXPERTS, EXPERTS, CAP, D).transpose(1, 0, 2, 3).reshape(EXPERTS, EXPERTS * CAP, D)
        back_gate = gate_grad_rows.reshape(EXPERTS, EXPERTS, CAP).transpose(1, 0, 2).reshape(EXPERTS, EXPERTS * CAP)

        def collect(rows_back, gates_back, idx):
            picked = rows_back[idx].astype(jnp.float32).reshape(TOK_DEV, TOP, D)
            return (lax.optimization_barrier(jnp.sum(picked, axis=1)).astype(jnp.bfloat16), gates_back[idx].reshape(TOK_DEV, TOP))
        tok_grad, gate_grad = jax.vmap(collect)(back_rows, back_gate, slot_index)
        token_grads.append(tok_grad.reshape(EXPERTS * TOK_DEV, D))
        gate_grads.append(gate_grad.reshape(EXPERTS * TOK_DEV, TOP))
    grad_scale = 1.0 / jnp.sqrt(jnp.float32(ROUTE_COUNT))
    grad_tokens = jnp.concatenate(token_grads, axis=0)
    grad_gates = jnp.concatenate(gate_grads, axis=0)
    return (grad_tokens, grad_gates, total_gu * grad_scale, total_down * grad_scale)
```

```python
import jax
import jax.numpy as jnp
import numpy as np
from jax import lax
from jax.sharding import PartitionSpec as P

BF16 = jnp.bfloat16
F32 = jnp.float32


def dot(a, b, contract):
    return lax.dot_general(a, b, (contract, ((), ())), preferred_element_type=F32)


def on_device(tokens, out_grad, routes, gate_weights, saved_preacts, gate_up, down_proj):
    experts = lax.axis_size("expert")
    groups = lax.axis_size("dp")
    tok_rows, top = routes.shape
    width = tokens.shape[1]
    part = width // groups
    slot_total = saved_preacts.shape[2]
    capacity = slot_total // experts
    hidden = saved_preacts.shape[3] // 2
    hidden_part = hidden // groups
    line = 4
    plane = experts // line
    me = lax.axis_index("expert")
    replica = lax.axis_index("dp")
    hi, lo = me // plane, me % plane

    def along_line(v, k):
        if k % line == 0:
            return v
        return lax.ppermute(v, "expert", [(i, (i + k * plane) % experts) for i in range(experts)])

    def in_plane(v, k):
        if k == 0:
            return v
        return lax.ppermute(v, "expert", [(i, i ^ k) for i in range(experts)])

    def over_dp(v, j):
        if j == 0:
            return v
        return lax.ppermute(v, "dp", [(i, (i + j) % groups) for i in range(groups)])

    def part_of(v, index, size, axis):
        return lax.dynamic_slice_in_dim(v, index * size, size, axis)

    def after(v, *others):
        return lax.optimization_barrier((v, *others))[0]

    names = jnp.arange(experts, dtype=jnp.int32)
    hits = routes[:, :, None] == names[None, None, :]
    routed = jnp.any(hits, axis=1)
    gates = jnp.sum(jnp.where(hits, gate_weights.astype(F32)[:, :, None], 0.0), axis=1)
    earlier = np.tril(np.ones((tok_rows, tok_rows), np.float32), -1)
    before = dot(jnp.asarray(earlier, BF16), routed.astype(BF16), ((1,), (0,)))
    places = jnp.where(routed, before + 1.0, 0.0)
    lanes = -(-2 * experts // 128) * 128
    marks = jnp.concatenate([places, gates], axis=1).astype(BF16)
    marks = jnp.pad(marks, ((0, 0), (0, lanes - 2 * experts)))
    lane = jnp.arange(lanes, dtype=jnp.int32)

    piece = -(-line * capacity // 8) * 8
    half = plane // 2 * piece
    inner = np.arange(piece)
    inside = inner < line * capacity
    wanted = np.full((piece, line), -1.0, np.float32)
    wanted[inner[inside], inner[inside] // capacity] = inner[inside] % capacity + 1
    wanted = jnp.asarray(wanted, BF16)
    partner = jnp.arange(plane, dtype=jnp.int32)
    partner_lane = (hi * plane + (lo ^ partner))[:, None] == lane[None, :]
    partner_lane = partner_lane.astype(BF16)

    def picker(held):
        seen = dot(partner_lane, held, ((1,), (1,))).astype(BF16)
        seen = seen.reshape(plane, 1, line, tok_rows)
        hit = seen == wanted[None, :, :, None]
        return hit.astype(BF16).reshape(plane * piece, line * tok_rows)

    def pick(p, held):
        return dot(p, held, ((1,), (0,))).astype(BF16)

    def lines(v):
        return [along_line(v, k) for k in range(line)]

    def stack(values):
        return jnp.concatenate(values, axis=0)

    def block(v, k):
        return v[k * piece : (k + 1) * piece]

    def exchange(v, partners):
        return [in_plane(block(v, k), k) for k in partners]

    everyone = range(plane)

    cols = width // 2
    down_got = [over_dp(down_proj[0], j) for j in range(groups)]
    marks_line = lines(marks)
    dy_first = lines(out_grad[:, :cols])

    step = jnp.asarray(inner // capacity, jnp.int32)
    source = (hi - step) % line * plane + (lo ^ partner[:, None])
    order = jnp.where(jnp.asarray(inside), source * capacity + jnp.asarray(inner % capacity), -1)
    reorder = order.reshape(-1)[:, None] == jnp.arange(slot_total, dtype=jnp.int32)[None, :]
    saved_rows = pick(reorder.astype(BF16), saved_preacts[0, 0])
    held_marks = stack(marks_line)
    own_picker = picker(after(held_marks, saved_rows))

    dy_second = lines(after(out_grad[:, cols:], *dy_first))
    picked_first = pick(after(own_picker, *dy_first), stack(dy_first))
    rows_first = exchange(picked_first, everyone)

    down_got, picked_first = lax.optimization_barrier((down_got, picked_first))
    down_full = jnp.zeros((hidden, width), BF16)
    for j in range(groups):
        down_full = lax.dynamic_update_slice_in_dim(
            down_full, down_got[j], (replica - j) % groups * hidden_part, 0
        )
    x_parts = [part_of(tokens, (replica + j) % groups, part, 1) for j in range(groups)]
    x_others = [
        over_dp(jnp.concatenate([x_parts[j], marks], axis=1), j) for j in range(1, groups)
    ]

    second_in = jnp.concatenate([stack(dy_second), held_marks], axis=1)
    picked_second = pick(after(own_picker, picked_first, down_full), second_in)
    rows_second = exchange(picked_second, everyone)
    x_own_line = lines(after(x_parts[0], *dy_second))

    dy_a = stack(rows_first)
    grad_a = dot(after(dy_a, picked_second), down_full[:, :cols], ((1,), (1,)))
    x_others_line = [lines(after(v, grad_a)) for v in x_others]
    rows_second = stack(rows_second)
    dy_b = rows_second[:, :cols]
    own_lane = (lane == experts + me).astype(F32)
    g_rows = jnp.sum(rows_second[:, cols:].astype(F32) * own_lane, axis=1, keepdims=True)

    def activation(at, previous):
        saved = after(saved_rows, *previous)[at]
        gate_pre = saved[:, :hidden].astype(F32)
        up_pre = saved[:, hidden:].astype(F32)
        sigmoid_gate = jax.nn.sigmoid(gate_pre)
        act = (gate_pre * sigmoid_gate * up_pre).astype(BF16)
        act_grad = grad_a[at] + dot(dy_b[at], down_full[:, cols:], ((1,), (1,)))
        gate_sums = jnp.sum(act.astype(F32) * act_grad, axis=1, keepdims=True)
        gate_sums = (gate_sums / jnp.sqrt(F32(width))).astype(BF16)
        scaled_grad = g_rows[at] * act_grad
        grad_gate = scaled_grad * up_pre * sigmoid_gate * (1.0 + gate_pre * (1.0 - sigmoid_gate))
        grad_up = scaled_grad * gate_pre * sigmoid_gate
        return jnp.concatenate([grad_gate, grad_up], axis=1).astype(BF16), gate_sums, act

    far, far_sums, far_act = activation(slice(half, None), [grad_a])
    near, near_sums, near_act = activation(slice(0, half), [far])

    far_got = [over_dp(far, j) for j in range(1, groups)]
    near_got = [over_dp(after(near, *far_got), j) for j in range(1, groups)]

    def back_rows(v):
        return dot(v, gate_up[0], ((1,), (1,))).astype(BF16)

    def combine(p, back):
        dense = dot(p, back, ((0,), (0,))).astype(BF16)
        return [dense[k * tok_rows : (k + 1) * tok_rows] for k in range(line)]

    def total(values):
        result = values[0].astype(F32)
        for k in range(1, line):
            result = result + along_line(values[k], -k).astype(F32)
        return result

    x_own_line, _ = lax.optimization_barrier((x_own_line, near))
    x_own_picked = pick(own_picker, stack(x_own_line))
    x_own = exchange(x_own_picked, everyone)
    expert_lane = (lane == me).astype(F32)
    own_back = stack([back_rows(after(near, x_own_picked)), back_rows(after(far, x_own_picked))])
    own_sums = stack([near_sums, far_sums]).astype(F32) * expert_lane
    own_back = jnp.concatenate([own_back, own_sums.astype(BF16)], axis=1)
    own_back_got = exchange(own_back, everyone)

    act_late = after(stack([near_act, far_act]), own_back)
    scaled_dy = [(g_rows * v.astype(F32)).astype(BF16) for v in (dy_a, dy_b)]
    grad_dn_full = jnp.concatenate([dot(act_late, v, ((0,), (0,))) for v in scaled_dy], axis=1)

    x_pickers, x_picked = [], []
    for j in range(1, groups):
        held = stack(x_others_line[j - 1])
        x_pickers.append(picker(after(held[:, part:], grad_dn_full)))
        x_picked.append(pick(x_pickers[-1], held[:, :part]))
    far_back = []
    for v in far_got:
        far_rows = back_rows(after(v, *x_picked))
        far_back += [[in_plane(block(far_rows, k - plane // 2), k) for k in everyone if 2 * k >= plane]]
    own_dense = combine(own_picker, after(stack(own_back_got), far_rows))
    own_total = total(own_dense)
    x_other = [exchange(after(v, *far_back[-1]), everyone) for v in x_picked]

    sent = [
        part_of(grad_dn_full, (replica + j) % groups, hidden_part, 0).astype(BF16)
        for j in range(1, groups)
    ]
    sent = [over_dp(after(sent[j - 1], *near_got), j) for j in range(1, groups)]
    others = []
    for j in range(1, groups):
        near_rows = back_rows(after(near_got[j - 1], *far_back[-1], own_dense[0]))
        near_back = [in_plane(block(near_rows, k), k) for k in everyone if 2 * k < plane]
        others.append(combine(x_pickers[j - 1], stack(near_back + far_back[j - 1])))

    grad_scale = 1.0 / jnp.sqrt(F32(groups * tok_rows * top))
    whole = [stack([near, far])] + [stack([a, b]) for a, b in zip(near_got, far_got)]
    x_all = [stack(x_own)] + [stack(v) for v in x_other]
    x_all[0] = after(x_all[0], others[-1][0])
    grad_gu = 0.0
    for x_rows, grads in zip(x_all, whole):
        grad_gu = grad_gu + dot(x_rows, grads, ((0,), (0,)))
    grad_gu = grad_gu * grad_scale

    totals = [after(total(v), *sent) for v in others]
    others = [over_dp(v.astype(BF16), groups - 1 - j) for j, v in enumerate(totals)]
    grad_dn = part_of(grad_dn_full, replica, hidden_part, 0)
    for v in sent:
        grad_dn = grad_dn + v.astype(F32)
    grad_dn = grad_dn * grad_scale

    grad_tokens = jnp.zeros((tok_rows, width), BF16)
    grad_tokens = lax.dynamic_update_slice_in_dim(
        grad_tokens, own_total[:, :part].astype(BF16), replica * part, 1
    )
    for j in range(1, groups):
        grad_tokens = lax.dynamic_update_slice_in_dim(
            grad_tokens, others[j - 1], (replica + j) % groups * part, 1
        )

    found = routes[:, :, None] == names[None, None, :]
    grad_gates = jnp.sum(jnp.where(found, own_total[:, None, part : part + experts], 0.0), axis=2)
    grad_gates = grad_gates.astype(BF16)

    return (grad_tokens, grad_gates, grad_gu[None], grad_dn[None])


def solution(mesh):
    in_specs = (
        P(("dp", "expert"), None),
        P(("dp", "expert"), None),
        P(("dp", "expert"), None),
        P(("dp", "expert"), None),
        P("dp", "expert", None, None),
        P("expert", "dp", None),
        P("expert", "dp", None),
    )
    out_specs = (
        P(("dp", "expert"), None),
        P(("dp", "expert"), None),
        P("expert", "dp", None),
        P("expert", "dp", None),
    )
    return jax.shard_map(
        on_device, mesh=mesh, in_specs=in_specs, out_specs=out_specs, check_vma=False
    )
```

```python
import jax
import jax.numpy as jnp
import numpy as np
from jax import lax
from jax.sharding import PartitionSpec as P

BF16 = jnp.bfloat16
F32 = jnp.float32


def dot(a, b, contract):
    return lax.dot_general(a, b, (contract, ((), ())), preferred_element_type=F32)


def on_device(tokens, out_grad, routes, gate_weights, saved_preacts, gate_up, down_proj):
    experts = lax.axis_size("expert")
    groups = lax.axis_size("dp")
    tok_rows, top = routes.shape
    width = tokens.shape[1]
    part = width // groups
    slot_total = saved_preacts.shape[2]
    capacity = slot_total // experts
    hidden = saved_preacts.shape[3] // 2
    hidden_part = hidden // groups
    line = 4
    plane = experts // line
    me = lax.axis_index("expert")
    replica = lax.axis_index("dp")
    hi, lo = me // plane, me % plane

    def along_line(v, k):
        if k % line == 0:
            return v
        return lax.ppermute(v, "expert", [(i, (i + k * plane) % experts) for i in range(experts)])

    def in_plane(v, k):
        if k == 0:
            return v
        return lax.ppermute(v, "expert", [(i, i ^ k) for i in range(experts)])

    def over_dp(v, j):
        if j == 0:
            return v
        return lax.ppermute(v, "dp", [(i, (i + j) % groups) for i in range(groups)])

    def part_of(v, index, size, axis):
        return lax.dynamic_slice_in_dim(v, index * size, size, axis)

    def follow(v, *others):
        for other in others:
            v = v + (other[:1, :1].astype(F32) * 0.0).astype(v.dtype)
        return v

    names = jnp.arange(experts, dtype=jnp.int32)
    hits = routes[:, :, None] == names[None, None, :]
    routed = jnp.any(hits, axis=1)
    gates = jnp.sum(jnp.where(hits, gate_weights.astype(F32)[:, :, None], 0.0), axis=1)
    earlier = np.tril(np.ones((tok_rows, tok_rows), np.float32), -1)
    before = dot(jnp.asarray(earlier, BF16), routed.astype(BF16), ((1,), (0,)))
    places = jnp.where(routed, before + 1.0, 0.0)
    lanes = -(-2 * experts // 128) * 128
    marks = jnp.concatenate([places, gates], axis=1).astype(BF16)
    marks = jnp.pad(marks, ((0, 0), (0, lanes - 2 * experts)))
    lane = jnp.arange(lanes, dtype=jnp.int32)

    piece = -(-line * capacity // 8) * 8
    inner = np.arange(piece)
    inside = inner < line * capacity
    wanted = np.full((piece, line), -1.0, np.float32)
    wanted[inner[inside], inner[inside] // capacity] = inner[inside] % capacity + 1
    wanted = jnp.asarray(wanted, BF16)
    partner = jnp.arange(plane, dtype=jnp.int32)
    partner_lane = (hi * plane + (lo ^ partner))[:, None] == lane[None, :]
    partner_lane = partner_lane.astype(BF16)

    def picker(held):
        seen = dot(partner_lane, held, ((1,), (1,))).astype(BF16)
        seen = seen.reshape(plane, 1, line, tok_rows)
        hit = seen == wanted[None, :, :, None]
        return hit.astype(BF16).reshape(plane * piece, line * tok_rows)

    def pick(p, held):
        return dot(p, held, ((1,), (0,))).astype(BF16)

    def lines(v):
        return [along_line(v, k) for k in range(line)]

    def stack(values):
        return jnp.concatenate(values, axis=0)

    def block(v, k):
        return v[k * piece : (k + 1) * piece]

    def exchange(v, partners):
        return [in_plane(block(v, k), k) for k in partners]

    everyone = range(plane)

    cols = width // 2
    down_got = [over_dp(down_proj[0], j) for j in range(groups)]
    marks_line = lines(marks)
    dy_first = lines(out_grad[:, :cols])

    step = jnp.asarray(inner // capacity, jnp.int32)
    source = (hi - step) % line * plane + (lo ^ partner[:, None])
    order = jnp.where(jnp.asarray(inside), source * capacity + jnp.asarray(inner % capacity), -1)
    reorder = order.reshape(-1)[:, None] == jnp.arange(slot_total, dtype=jnp.int32)[None, :]
    saved_rows = pick(reorder.astype(BF16), saved_preacts[0, 0])
    held_marks = stack(marks_line)
    own_picker = picker(held_marks)

    dy_second = lines(follow(out_grad[:, cols:], dy_first[1], dy_first[2]))
    picked_first = pick(own_picker, stack(dy_first))
    rows_first = exchange(picked_first, everyone)

    down_full = jnp.zeros((hidden, width), BF16)
    for j in range(groups):
        down_full = lax.dynamic_update_slice_in_dim(
            down_full, down_got[j], (replica - j) % groups * hidden_part, 0
        )
    x_parts = [part_of(tokens, (replica + j) % groups, part, 1) for j in range(groups)]
    x_others = [
        over_dp(jnp.concatenate([x_parts[j], marks], axis=1), j) for j in range(1, groups)
    ]

    dy_a = stack(rows_first)
    grad_a = dot(dy_a, down_full[:, :cols], ((1,), (1,)))
    second_in = jnp.concatenate([stack(dy_second), follow(held_marks, grad_a, *x_others)], axis=1)
    picked_second = pick(own_picker, second_in)
    rows_second = exchange(picked_second, everyone)
    x_own_line = lines(follow(x_parts[0], rows_second[1]))

    rows_second = stack(rows_second)
    dy_b = rows_second[:, :cols]
    own_lane = (lane == experts + me).astype(F32)
    g_rows = jnp.sum(rows_second[:, cols:].astype(F32) * own_lane, axis=1, keepdims=True)

    gate_pre = saved_rows[:, :hidden].astype(F32)
    up_pre = saved_rows[:, hidden:].astype(F32)
    sigmoid_gate = jax.nn.sigmoid(gate_pre)
    act = (gate_pre * sigmoid_gate * up_pre).astype(BF16)
    act_grad = grad_a + dot(dy_b, down_full[:, cols:], ((1,), (1,)))
    gate_sums = jnp.sum(act.astype(F32) * act_grad, axis=1, keepdims=True)
    gate_sums = (gate_sums / jnp.sqrt(F32(width))).astype(BF16)
    scaled_grad = g_rows * act_grad
    grad_gate = scaled_grad * up_pre * sigmoid_gate * (1.0 + gate_pre * (1.0 - sigmoid_gate))
    grad_up = scaled_grad * gate_pre * sigmoid_gate
    pre_grad = jnp.concatenate([grad_gate, grad_up], axis=1).astype(BF16)
    pre_got = [over_dp(pre_grad, j) for j in range(1, groups)]

    def back_rows(v):
        return dot(v, gate_up[0], ((1,), (1,))).astype(BF16)

    def combine(p, back):
        dense = dot(p, back, ((0,), (0,))).astype(BF16)
        return [dense[k * tok_rows : (k + 1) * tok_rows] for k in range(line)]

    def moved(values):
        return [along_line(values[k], -k) for k in range(line)]

    def total(values):
        result = values[0].astype(F32)
        for v in values[1:]:
            result = result + v.astype(F32)
        return result

    expert_lane = (lane == me).astype(F32)
    own_sums = (gate_sums.astype(F32) * expert_lane).astype(BF16)
    own_back = jnp.concatenate([back_rows(pre_grad), own_sums], axis=1)
    x_others_line = [lines(follow(v, own_back)) for v in x_others]
    own_moved = moved(combine(own_picker, stack(exchange(own_back, everyone))))
    x_own = exchange(pick(own_picker, stack(x_own_line)), everyone)

    g_later = follow(g_rows, pre_grad)
    scaled_dy = [(g_later * v.astype(F32)).astype(BF16) for v in (dy_a, dy_b)]
    grad_dn_full = jnp.concatenate([dot(act, v, ((0,), (0,))) for v in scaled_dy], axis=1)

    sent = [
        part_of(grad_dn_full, (replica + j) % groups, hidden_part, 0).astype(BF16)
        for j in range(1, groups)
    ]
    sent = [over_dp(follow(v, pre_got[-1]), j + 1) for j, v in enumerate(sent)]
    x_other, others = [], []
    for v, lined in zip(pre_got, x_others_line):
        held = stack(lined)
        x_picker = picker(held[:, part:])
        back = stack(exchange(back_rows(v), everyone))
        others.append(combine(x_picker, follow(back, *sent, *own_moved[1:])))
        x_picked = follow(pick(x_picker, held[:, :part]), others[-1][0])
        x_other.append(exchange(x_picked, everyone))
    own_total = total(own_moved)

    grad_scale = 1.0 / jnp.sqrt(F32(groups * tok_rows * top))
    whole = pre_got + [pre_grad]
    x_all = [stack(v) for v in x_other] + [follow(stack(x_own), *sent)]
    grad_gu = 0.0
    for x_rows, grads in zip(x_all, whole):
        grad_gu = grad_gu + dot(x_rows, grads, ((0,), (0,)))
    grad_gu = grad_gu * grad_scale

    totals = [total(moved(v)) for v in others]
    others = [over_dp(v.astype(BF16), groups - 1 - j) for j, v in enumerate(totals)]
    grad_dn = part_of(grad_dn_full, replica, hidden_part, 0)
    for v in sent:
        grad_dn = grad_dn + v.astype(F32)
    grad_dn = grad_dn * grad_scale

    grad_tokens = jnp.zeros((tok_rows, width), BF16)
    grad_tokens = lax.dynamic_update_slice_in_dim(
        grad_tokens, own_total[:, :part].astype(BF16), replica * part, 1
    )
    for j in range(1, groups):
        grad_tokens = lax.dynamic_update_slice_in_dim(
            grad_tokens, others[j - 1], (replica + j) % groups * part, 1
        )

    found = routes[:, :, None] == names[None, None, :]
    grad_gates = jnp.sum(jnp.where(found, own_total[:, None, part : part + experts], 0.0), axis=2)
    grad_gates = grad_gates.astype(BF16)

    return (grad_tokens, grad_gates, grad_gu[None], grad_dn[None])


def solution(mesh):
    in_specs = (
        P(("dp", "expert"), None),
        P(("dp", "expert"), None),
        P(("dp", "expert"), None),
        P(("dp", "expert"), None),
        P("dp", "expert", None, None),
        P("expert", "dp", None),
        P("expert", "dp", None),
    )
    out_specs = (
        P(("dp", "expert"), None),
        P(("dp", "expert"), None),
        P("expert", "dp", None),
        P("expert", "dp", None),
    )
    return jax.shard_map(
        on_device, mesh=mesh, in_specs=in_specs, out_specs=out_specs, check_vma=False
    )
```

```python
import jax
import jax.numpy as jnp
import numpy as np
from jax import lax
from jax.sharding import PartitionSpec as P

BF16 = jnp.bfloat16
F32 = jnp.float32


def dot(a, b, contract):
    return lax.dot_general(a, b, (contract, ((), ())), preferred_element_type=F32)


def on_device(tokens, out_grad, routes, gate_weights, saved_preacts, gate_up, down_proj):
    experts = lax.axis_size("expert")
    groups = lax.axis_size("dp")
    tok_rows, top = routes.shape
    width = tokens.shape[1]
    part = width // groups
    slot_total = saved_preacts.shape[2]
    capacity = slot_total // experts
    hidden = saved_preacts.shape[3] // 2
    hidden_part = hidden // groups
    line = 4
    plane = experts // line
    me = lax.axis_index("expert")
    replica = lax.axis_index("dp")
    hi, lo = me // plane, me % plane

    def along_line(v, k):
        if k % line == 0:
            return v
        return lax.ppermute(v, "expert", [(i, (i + k * plane) % experts) for i in range(experts)])

    def in_plane(v, k):
        if k == 0:
            return v
        return lax.ppermute(v, "expert", [(i, i ^ k) for i in range(experts)])

    def over_dp(v, j):
        if j == 0:
            return v
        return lax.ppermute(v, "dp", [(i, (i + j) % groups) for i in range(groups)])

    def part_of(v, index, size, axis):
        return lax.dynamic_slice_in_dim(v, index * size, size, axis)

    def follow(v, *others):
        for other in others:
            v = v + (other[:1, :1].astype(F32) * 0.0).astype(v.dtype)
        return v

    names = jnp.arange(experts, dtype=jnp.int32)
    hits = routes[:, :, None] == names[None, None, :]
    routed = jnp.any(hits, axis=1)
    gates = jnp.sum(jnp.where(hits, gate_weights.astype(F32)[:, :, None], 0.0), axis=1)
    earlier = np.tril(np.ones((tok_rows, tok_rows), np.float32), -1)
    before = dot(jnp.asarray(earlier, BF16), routed.astype(BF16), ((1,), (0,)))
    places = jnp.where(routed, before + 1.0, 0.0)
    lanes = -(-2 * experts // 128) * 128
    marks = jnp.concatenate([places, gates], axis=1).astype(BF16)
    marks = jnp.pad(marks, ((0, 0), (0, lanes - 2 * experts)))
    lane = jnp.arange(lanes, dtype=jnp.int32)

    piece = -(-line * capacity // 8) * 8
    inner = np.arange(piece)
    inside = inner < line * capacity
    wanted = np.full((piece, line), -1.0, np.float32)
    wanted[inner[inside], inner[inside] // capacity] = inner[inside] % capacity + 1
    wanted = jnp.asarray(wanted, BF16)
    partner = jnp.arange(plane, dtype=jnp.int32)
    partner_lane = (hi * plane + (lo ^ partner))[:, None] == lane[None, :]
    partner_lane = partner_lane.astype(BF16)

    def picker(held):
        seen = dot(partner_lane, held, ((1,), (1,))).astype(BF16)
        seen = seen.reshape(plane, 1, line, tok_rows)
        hit = seen == wanted[None, :, :, None]
        return hit.astype(BF16).reshape(plane * piece, line * tok_rows)

    def pick(p, held):
        return dot(p, held, ((1,), (0,))).astype(BF16)

    def lines(v):
        return [along_line(v, k) for k in range(line)]

    def stack(values):
        return jnp.concatenate(values, axis=0)

    def block(v, k):
        return v[k * piece : (k + 1) * piece]

    def exchange(v, partners):
        return [in_plane(block(v, k), k) for k in partners]

    everyone = range(plane)

    cols = width // 2
    down_got = [over_dp(down_proj[0], j) for j in range(groups)]
    marks_line = lines(marks)
    dy_first = lines(out_grad[:, :cols])

    step = jnp.asarray(inner // capacity, jnp.int32)
    source = (hi - step) % line * plane + (lo ^ partner[:, None])
    order = jnp.where(jnp.asarray(inside), source * capacity + jnp.asarray(inner % capacity), -1)
    reorder = order.reshape(-1)[:, None] == jnp.arange(slot_total, dtype=jnp.int32)[None, :]
    saved_rows = pick(reorder.astype(BF16), saved_preacts[0, 0])
    held_marks = stack(marks_line)
    own_picker = picker(held_marks)

    dy_second = lines(follow(out_grad[:, cols:], dy_first[1], dy_first[2]))
    picked_first = pick(own_picker, stack(dy_first))
    rows_first = exchange(picked_first, everyone)

    down_full = jnp.zeros((hidden, width), BF16)
    for j in range(groups):
        down_full = lax.dynamic_update_slice_in_dim(
            down_full, down_got[j], (replica - j) % groups * hidden_part, 0
        )
    x_parts = [part_of(tokens, (replica + j) % groups, part, 1) for j in range(groups)]
    x_others = [
        over_dp(jnp.concatenate([x_parts[j], marks], axis=1), j) for j in range(1, groups)
    ]

    dy_a = stack(rows_first)
    grad_a = dot(dy_a, down_full[:, :cols], ((1,), (1,)))
    second_in = jnp.concatenate([stack(dy_second), follow(held_marks, grad_a, *x_others)], axis=1)
    picked_second = pick(own_picker, second_in)
    rows_second = exchange(picked_second, everyone)
    x_own_line = lines(follow(x_parts[0], rows_second[1]))

    rows_second = stack(rows_second)
    dy_b = rows_second[:, :cols]
    own_lane = (lane == experts + me).astype(F32)
    g_rows = jnp.sum(rows_second[:, cols:].astype(F32) * own_lane, axis=1, keepdims=True)

    gate_pre = saved_rows[:, :hidden].astype(F32)
    up_pre = saved_rows[:, hidden:].astype(F32)
    sigmoid_gate = jax.nn.sigmoid(gate_pre)
    act = (gate_pre * sigmoid_gate * up_pre).astype(BF16)
    act_grad = grad_a + dot(dy_b, down_full[:, cols:], ((1,), (1,)))
    gate_sums = jnp.sum(act.astype(F32) * act_grad, axis=1, keepdims=True)
    gate_sums = (gate_sums / jnp.sqrt(F32(width))).astype(BF16)
    scaled_grad = g_rows * act_grad
    grad_gate = scaled_grad * up_pre * sigmoid_gate * (1.0 + gate_pre * (1.0 - sigmoid_gate))
    grad_up = scaled_grad * gate_pre * sigmoid_gate
    pre_grad = jnp.concatenate([grad_gate, grad_up], axis=1).astype(BF16)
    pre_got = [over_dp(pre_grad, j) for j in range(1, groups)]

    def back_rows(v):
        return dot(v, gate_up[0], ((1,), (1,))).astype(BF16)

    def combine(p, back):
        dense = dot(p, back, ((0,), (0,))).astype(BF16)
        return [dense[k * tok_rows : (k + 1) * tok_rows] for k in range(line)]

    def moved(values):
        return [along_line(values[k], -k) for k in range(line)]

    def total(values):
        result = values[0].astype(F32)
        for v in values[1:]:
            result = result + v.astype(F32)
        return result

    expert_lane = (lane == me).astype(F32)
    own_sums = (gate_sums.astype(F32) * expert_lane).astype(BF16)
    own_back = jnp.concatenate([back_rows(pre_grad), own_sums], axis=1)
    own_got = exchange(own_back, everyone)
    x_others_line = [lines(follow(v, own_got[2])) for v in x_others]
    own_moved = moved(combine(own_picker, stack(own_got)))
    x_own = exchange(pick(own_picker, stack(x_own_line)), everyone)

    g_later = follow(g_rows, pre_grad)
    scaled_dy = [(g_later * v.astype(F32)).astype(BF16) for v in (dy_a, dy_b)]
    grad_dn_full = jnp.concatenate([dot(act, v, ((0,), (0,))) for v in scaled_dy], axis=1)

    sent = [
        part_of(grad_dn_full, (replica + j) % groups, hidden_part, 0).astype(BF16)
        for j in range(1, groups)
    ]
    sent = [over_dp(follow(v, pre_got[-1]), j + 1) for j, v in enumerate(sent)]
    x_other, others = [], []
    for v, lined in zip(pre_got, x_others_line):
        held = stack(lined)
        x_picker = picker(held[:, part:])
        back = stack(exchange(back_rows(v), everyone))
        others.append(combine(x_picker, follow(back, *sent, *own_moved[1:])))
        x_picked = follow(pick(x_picker, held[:, :part]), others[-1][0])
        x_other.append(exchange(x_picked, everyone))
    own_total = total(own_moved)

    grad_scale = 1.0 / jnp.sqrt(F32(groups * tok_rows * top))
    whole = pre_got + [pre_grad]
    x_all = [stack(v) for v in x_other] + [follow(stack(x_own), *sent)]
    grad_gu = 0.0
    for x_rows, grads in zip(x_all, whole):
        grad_gu = grad_gu + dot(x_rows, grads, ((0,), (0,)))
    grad_gu = grad_gu * grad_scale

    totals = [total(moved(v)) for v in others]
    others = [over_dp(v.astype(BF16), groups - 1 - j) for j, v in enumerate(totals)]
    grad_dn = part_of(grad_dn_full, replica, hidden_part, 0)
    for v in sent:
        grad_dn = grad_dn + v.astype(F32)
    grad_dn = grad_dn * grad_scale

    grad_tokens = jnp.zeros((tok_rows, width), BF16)
    grad_tokens = lax.dynamic_update_slice_in_dim(
        grad_tokens, own_total[:, :part].astype(BF16), replica * part, 1
    )
    for j in range(1, groups):
        grad_tokens = lax.dynamic_update_slice_in_dim(
            grad_tokens, others[j - 1], (replica + j) % groups * part, 1
        )

    found = routes[:, :, None] == names[None, None, :]
    grad_gates = jnp.sum(jnp.where(found, own_total[:, None, part : part + experts], 0.0), axis=2)
    grad_gates = grad_gates.astype(BF16)

    return (grad_tokens, grad_gates, grad_gu[None], grad_dn[None])


def solution(mesh):
    in_specs = (
        P(("dp", "expert"), None),
        P(("dp", "expert"), None),
        P(("dp", "expert"), None),
        P(("dp", "expert"), None),
        P("dp", "expert", None, None),
        P("expert", "dp", None),
        P("expert", "dp", None),
    )
    out_specs = (
        P(("dp", "expert"), None),
        P(("dp", "expert"), None),
        P("expert", "dp", None),
        P("expert", "dp", None),
    )
    return jax.shard_map(
        on_device, mesh=mesh, in_specs=in_specs, out_specs=out_specs, check_vma=False
    )
```
